512 devices in a mesh: member: 16 (over z), space: 32 (over x, y, core).
Axes of the slice: x: 4, y: 4, z: 16, core: 2. Of those that a mesh axis runs over, the one named last changes fastest.
Arguments:
- background_samples: float32 [80, 524288], P('member', 'space'), may hold values from -6 to 6
- measured_quantity: float32 [2, 32768], P(None, 'space'), may hold values from -6 to 6
- measurement_noise_variance: float32 [2, 32768], P(None, 'space'), may hold values from 0.25 to 2
- measured_grid_point: int32 [2, 32768], P(None, 'space'), may hold values from 0 to 16383
- measurement_sort: int32 [2, 32768], P(None, 'space'), may hold values from 0 to 3
- distance_damping_weights: float32 [4, 8], replicated, may hold values from 0.2 to 1
Outputs:
- analysis: float32 [80, 524288], P('member', 'space')
The draws below stay inside these ranges and needn't reach their ends.
Inputs may be any that keep to these rules, and one draw needn't show every extreme that they name: Observation j of a batch is owned by block j // 1024; measured_grid_point counts cells inside that block.
All inputs are finite; a program needn't handle non-finite values.
Results may differ from the reference program's by a relative error of at most 0.0003.
Values sent between devices are 32-bit elements; how exact they have to be, the bound alone decides.
No kernel may reach another device: no remote copies, remote signals or barrier semaphores. Data moves between devices by JAX's collectives and lax.ppermute only.
A program may use at most 128 MiB of HBM per device.

```python
import math
import jax
import jax.numpy as jnp
from jax import lax

SAMPLE_COUNT = 80
OBS_BLK = 1024
BATCHES = 2
CLASSES = 4
TAB = 8
BLOCK = 16384
BUCKET = 2048
GRID_POINTS = 524288
OBS = 32768
N_SPACE = 32


def place_ends(values, stream_key, low, top_value):
    place = [jax.random.randint(jax.random.fold_in(stream_key, axis), (), 0, length) for axis, length in enumerate(values.shape)]
    widest = values.shape.index(max(values.shape))
    neighbour = place[:widest] + [(place[widest] + 1) % values.shape[widest]] + place[widest + 1:]
    return values.at[tuple(place)].set(low).at[tuple(neighbour)].set(top_value)


def shard_levels(rng, shape, cuts, least, largest):
    gain = 1.0
    for axis_at, parts in cuts:
        draws = jax.random.uniform(jax.random.fold_in(jax.random.fold_in(rng, 6), axis_at), (parts,), jnp.float32, least / len(cuts), largest / len(cuts))
        gain = gain * jnp.repeat(jnp.exp(draws), shape[axis_at] // parts).reshape((-1,) + (1,) * (len(shape) - 1 - axis_at))
    return gain


def scatter_about(rng, shape, width, limit, split=(), held_as=jnp.bfloat16):
    entries = jax.random.normal(rng, shape, jnp.float32) * width
    if len(split) > 0:
        entries = shard_levels(rng, shape, split, -0.22, 0.18) * entries
    return jnp.clip(entries, min=-limit, max=limit).astype(held_as)


def setup_inputs(seed: int = 0) -> dict:
    streams_of = jax.random.split(jax.random.key(seed), 7)
    return {
        "background_samples": scatter_about(streams_of[0], (SAMPLE_COUNT, GRID_POINTS), 1.0, 6.0, ((0, 16), (1, 32)), jnp.float32),
        "measured_quantity": scatter_about(streams_of[1], (BATCHES, OBS), 1.0, 6.0, ((1, 32),), jnp.float32),
        "measurement_noise_variance": jnp.clip(jnp.exp(math.log(2.0) - 2.0794415 * jax.random.uniform(streams_of[2], (BATCHES, OBS), jnp.float32) ** shard_levels(streams_of[2], (BATCHES, OBS), ((1, 32),), -0.2, 0.2)), 0.25, 2.0),
        "measured_grid_point": place_ends(jax.random.randint(streams_of[3], (BATCHES, OBS), 0, BLOCK), jax.random.fold_in(streams_of[3], 1), 0, BLOCK - 1).astype(jnp.int32),
        "measurement_sort": place_ends(jax.random.randint(streams_of[4], (BATCHES, OBS), 0, CLASSES), jax.random.fold_in(streams_of[4], 1), 0, CLASSES - 1).astype(jnp.int32),
        "distance_damping_weights": jnp.clip(jax.random.uniform(streams_of[5], (CLASSES, TAB), jnp.float32, 0.2, 1.0), 0.2, 1.0),
    }


precise = lax.Precision.HIGHEST

def taper_rows(distance_damping_weights, classes):
    onehot = (classes[None, :] == jnp.arange(distance_damping_weights.shape[0], dtype=jnp.int32)[:, None]).astype(jnp.float32)
    return jnp.dot(distance_damping_weights.T, onehot, precision=precise)

def assimilate(sample_matrix, positions, bundle, total_cells, bucket, sections):
    sample_lines = sample_matrix.shape[0]
    levels = bundle.shape[0] - sample_lines - 3
    obs_width = bundle.shape[1] // sections
    cell_mean = lax.optimization_barrier(jnp.mean(sample_matrix, axis=0))
    cell_dev = sample_matrix - cell_mean[None, :]
    mean_step = jnp.zeros_like(cell_mean)
    dev_step = jnp.zeros_like(cell_dev)
    for section in range(sections):
        chosen = bundle[:, section * obs_width:(section + 1) * obs_width]
        picked = chosen[:sample_lines]
        values = chosen[sample_lines]
        errors = chosen[sample_lines + 1]
        obs_where = chosen[sample_lines + 2]
        obs_taper = chosen[sample_lines + 3:]
        obs_mean = lax.optimization_barrier(jnp.mean(picked, axis=0))
        obs_dev = picked - obs_mean[None, :]
        obs_spread = lax.optimization_barrier(jnp.sum(obs_dev * obs_dev, axis=0)) / (sample_lines - 1)
        offset_abs = jnp.abs(positions[:, None] - obs_where[None, :])
        distance = jnp.minimum(offset_abs, total_cells - offset_abs)
        weights = jnp.zeros_like(distance)
        for level in range(levels):
            inside = (distance >= level * bucket) & (distance < (level + 1) * bucket)
            weights = weights + jnp.where(inside, obs_taper[level][None, :], 0.0)
        covariance = lax.dot_general(cell_dev, obs_dev, (((0,), (0,)), ((), ())), precision=precise) / (sample_lines - 1)
        kalman_gain = weights * covariance / (obs_spread + errors)[None, :]
        shrink = 1.0 / (1.0 + jnp.sqrt(errors / (obs_spread + errors)))
        mean_step = mean_step + jnp.dot(kalman_gain, values - obs_mean, precision=precise)
        dev_step = dev_step + lax.dot_general(obs_dev, kalman_gain * shrink[None, :], (((1,), (1,)), ((), ())), precision=precise)
    return (cell_mean + mean_step)[None, :] + (cell_dev - dev_step)

def reference(background_samples, measured_quantity, measurement_noise_variance, measured_grid_point, measurement_sort, distance_damping_weights):
    sample_lines = background_samples.shape[0]
    total_cells = BLOCK * N_SPACE
    sample_matrix = background_samples
    starts = jnp.arange(N_SPACE, dtype=jnp.int32) * BLOCK
    for batch in range(BATCHES):
        obs_global = (measured_grid_point[batch].reshape(N_SPACE, OBS_BLK) + starts[:, None]).reshape(-1).astype(jnp.int32)
        picked = jnp.take(sample_matrix, obs_global, axis=1)
        bundle = jnp.concatenate([picked, measured_quantity[batch][None, :], measurement_noise_variance[batch][None, :], obs_global.astype(jnp.float32)[None, :], taper_rows(distance_damping_weights, measurement_sort[batch])], axis=0)
        grouped = bundle.reshape(bundle.shape[0], N_SPACE, OBS_BLK)
        current = sample_matrix

        def one_block(block_at):
            chosen_blocks = ((block_at + jnp.array([N_SPACE - 1, 0, 1], dtype=jnp.int32)) % N_SPACE).astype(jnp.int32)
            beside_all = jnp.take(grouped, chosen_blocks, axis=1).reshape(grouped.shape[0], 3 * OBS_BLK)
            cells_here = lax.dynamic_slice_in_dim(current, (block_at * BLOCK).astype(jnp.int32), BLOCK, 1)
            positions = (block_at * BLOCK + jnp.arange(BLOCK, dtype=jnp.int32)).astype(jnp.float32)
            return assimilate(cells_here, positions, beside_all, total_cells, BUCKET, 3)
        updated = lax.map(one_block, jnp.arange(N_SPACE, dtype=jnp.int32))
        sample_matrix = jnp.transpose(updated, (1, 0, 2)).reshape(sample_lines, total_cells)
    return sample_matrix
```

```python
import jax
import jax.numpy as jnp
from jax import lax
from jax.experimental import pallas as pl
from jax.experimental.pallas import tpu as pltpu
from jax.sharding import PartitionSpec as P

MEMBERS = 80
CELLS = 1024
BLOCK = 16384
BIN_BITS = 11
BINS = 8
CLASSES = 4
ROWS = 640
BUNDLE = 672
TILE = 256
TILES = 12
f32 = jnp.float32
bf16 = jnp.bfloat16
VM = pl.BlockSpec(memory_space=pltpu.VMEM)
SM = pl.BlockSpec(memory_space=pltpu.SMEM)
PARAMS = pltpu.CompilerParams(vmem_limit_bytes=48 * 1024 * 1024)


def split(value):
    high = value.astype(bf16)
    low = (value - high.astype(f32)).astype(bf16)
    return high, low


def pick_kernel(x_ref, gp_ref, send_ref, picks_ref, parts_ref):
    for c in range(128):
        d, r = c // 8, c % 8
        slab = x_ref[:, c * 128 : (c + 1) * 128]
        send_ref[pl.ds(d * 40 + r, 5, stride=8), :] = slab
    lane = lax.broadcasted_iota(jnp.int32, (128, 128), 0)
    for m in range(5):
        slabs = jnp.concatenate([send_ref[d * 40 + m * 8 : d * 40 + m * 8 + 8, :] for d in range(16)], axis=0)
        high, low = split(slabs)
        parts_ref[m * 128 : (m + 1) * 128, :128] = high
        parts_ref[m * 128 : (m + 1) * 128, 128:] = low
    for b in range(2):
        for r in range(8):
            cell = gp_ref[b : b + 1, r * 128 : (r + 1) * 128]
            onehot = jnp.where((cell & 127) == lane, 1.0, 0.0).astype(bf16)
            found = jnp.dot(
                parts_ref[...], jnp.concatenate([onehot, onehot], axis=0), preferred_element_type=f32
            )
            here = lane == (cell >> 7)
            for m in range(5):
                value = jnp.where(here, found[m * 128 : (m + 1) * 128, :], 0.0)
                picks_ref[b * 40 + m * 8 + r : b * 40 + m * 8 + r + 1, :] = jnp.sum(value, axis=0, keepdims=True)


def pick(samples, grid_point):
    return pl.pallas_call(
        pick_kernel,
        out_shape=(jax.ShapeDtypeStruct((ROWS, 128), f32), jax.ShapeDtypeStruct((80, 128), f32)),
        in_specs=[VM, VM],
        out_specs=(VM, VM),
        scratch_shapes=[pltpu.VMEM((640, 256), bf16)],
        compiler_params=PARAMS,
        name="pick",
    )(samples, grid_point)


def bundle_kernel(gathered_ref, par_ref, bundle_ref, cells_ref):
    for k in range(16):
        bundle_ref[k * 40 : (k + 1) * 40, :] = gathered_ref[k * 80 : k * 80 + 40, :]
        cells_ref[k * 40 : (k + 1) * 40, :] = gathered_ref[k * 80 + 40 : k * 80 + 80, :]
    bundle_ref[ROWS:BUNDLE, :] = par_ref[...]


def make_bundle(gathered, par):
    return pl.pallas_call(
        bundle_kernel,
        out_shape=(jax.ShapeDtypeStruct((BUNDLE, 128), f32), jax.ShapeDtypeStruct((ROWS, 128), f32)),
        in_specs=[VM, VM],
        out_specs=(VM, VM),
        compiler_params=PARAMS,
        name="bundle",
    )(gathered, par)


def taper_of(classes, tab_ref):
    rows = []
    for b in range(BINS):
        row = jnp.zeros(classes.shape, f32)
        for c in range(CLASSES):
            row = jnp.where(classes == c, tab_ref[c, b], row)
        rows.append(row)
    return rows


def prepare_section(sec, ref, where, tab_ref, d3_ref, a2_ref, rows_ref, bulk):
    place = ref[656:664, :].astype(jnp.int32)
    classes = ref[664:672, :].astype(jnp.int32)
    taper = taper_of(classes, tab_ref)
    if bulk:
        first = where - place
        rising = first >= 0
        dist = jnp.abs(first)
        bin0 = dist >> BIN_BITS
        inner = dist & ((1 << BIN_BITS) - 1)
        turn = jnp.where(rising, (1 << BIN_BITS) - inner, inner + 1)
        bin1 = jnp.where(rising, bin0 + 1, jnp.maximum(bin0 - 1, 0))
        before = jnp.zeros(classes.shape, f32)
        after = jnp.zeros(classes.shape, f32)
        for b in range(BINS):
            before = jnp.where(bin0 == b, taper[b], before)
            after = jnp.where(bin1 == b, taper[b], after)
    else:
        shifted = place - where
    for r in range(8):
        tile, col = (sec * 8 + r) // 2, ((sec * 8 + r) % 2) * 128
        cols = slice(col, col + 128)
        prior = ref[pl.ds(r, MEMBERS, stride=8), :]
        mean = jnp.sum(prior, axis=0, keepdims=True) / MEMBERS
        dev = prior - mean
        spread = jnp.sum(dev * dev, axis=0, keepdims=True) / (MEMBERS - 1)
        value = ref[640 + r : 641 + r, :]
        error = ref[648 + r : 649 + r, :]
        total = spread + error
        scale = 1.0 / (total * (MEMBERS - 1))
        shrink = 1.0 / (1.0 + jnp.sqrt(error / total))
        step = (value - mean) - shrink * dev
        high, low = split(dev)
        d3_ref[tile, 0:80, cols] = high
        d3_ref[tile, 80:160, cols] = high
        d3_ref[tile, 160:240, cols] = low
        d3_ref[tile, 240:256, cols] = jnp.zeros((16, 128), bf16)
        high, low = split(step)
        pad = jnp.zeros((48, 128), bf16)
        a2_ref[tile, 0:80, cols] = high
        a2_ref[tile, 80:128, cols] = pad
        a2_ref[tile, 128:208, cols] = low
        a2_ref[tile, 208:256, cols] = pad
        full = (8, 128)
        if bulk:
            rows_ref[tile, 0:8, cols] = jnp.broadcast_to(turn[r : r + 1, :].astype(f32), full)
            rows_ref[tile, 8:16, cols] = jnp.broadcast_to(before[r : r + 1, :] * scale, full)
            rows_ref[tile, 16:24, cols] = jnp.broadcast_to(after[r : r + 1, :] * scale, full)
        else:
            rows_ref[tile, 0:8, cols] = jnp.broadcast_to(shifted[r : r + 1, :].astype(f32), full)
            table = jnp.concatenate([taper[b][r : r + 1, :] * scale for b in range(BINS)], axis=0)
            rows_ref[tile, 8:16, cols] = table


def update_kernel(
    bulk, at_ref, tab_ref, x_ref, pos_ref, own_ref, side_ref, off_ref, out_ref, e3_ref, d3_ref, a2_ref, rows_ref, acc_ref, posb_ref
):
    start = at_ref[0] if bulk else 0
    for r in range(8):
        cells = x_ref[pl.ds(r, MEMBERS, stride=8), :]
        dev = cells - jnp.sum(cells, axis=0, keepdims=True) / MEMBERS
        high = dev.astype(bf16).astype(f32)
        low = dev - high
        stacked = jnp.concatenate([high, low, high, jnp.zeros((16, 128), f32)], axis=0)
        e3_ref[r * 128 : (r + 1) * 128, :] = stacked.T.astype(bf16)
        if not bulk:
            row = jnp.broadcast_to(pos_ref[r : r + 1, :], (128, 128))
            posb_ref[r * 128 : (r + 1) * 128, :] = row.T
    for sec, (ref, offset) in enumerate(((own_ref, 0), (side_ref, at_ref[1]), (off_ref, at_ref[2]))):
        prepare_section(sec, ref, start - offset, tab_ref, d3_ref, a2_ref, rows_ref, bulk)
    acc_ref[...] = jnp.zeros_like(acc_ref)
    part = 256

    def tile_step(tile, carry):
        for ic in range(CELLS // part):
            rows = slice(ic * part, (ic + 1) * part)
            cov = jnp.dot(e3_ref[rows, :], d3_ref[tile], preferred_element_type=f32)
            cov = cov.reshape(part // 8, 8, TILE)
            if bulk:
                at = lax.broadcasted_iota(jnp.int32, (part, TILE), 0).astype(f32).reshape(part // 8, 8, TILE) + float(ic * part)
                turn = rows_ref[tile, 0:8, :][None]
                weight = jnp.where(at >= turn, rows_ref[tile, 16:24, :][None], rows_ref[tile, 8:16, :][None])
            else:
                halves = []
                for h in range(2):
                    cols = slice(h * 128, (h + 1) * 128)
                    place = rows_ref[tile, 0:8, cols]
                    table = rows_ref[tile, 8:16, cols]
                    slabs = []
                    for g in range(part // 8):
                        pos = posb_ref[ic * part + g * 8 : ic * part + g * 8 + 8, :]
                        dist = jnp.abs(pos - place).astype(jnp.int32)
                        level = dist >> BIN_BITS
                        got = jnp.take_along_axis(table, level & (BINS - 1), axis=0, mode="promise_in_bounds")
                        slabs.append(jnp.where(level < BINS, got, 0.0)[None])
                    halves.append(jnp.concatenate(slabs, axis=0))
                weight = jnp.concatenate(halves, axis=2)
            gain = (weight * cov).reshape(part, TILE)
            high, low = split(gain)
            nt = (((1,), (1,)), ((), ()))
            acc_ref[rows, :] += lax.dot_general(high, a2_ref[tile], nt, preferred_element_type=f32)
            acc_ref[rows, :128] += lax.dot_general(low, a2_ref[tile, 0:128, :], nt, preferred_element_type=f32)
        return carry

    lax.fori_loop(0, TILES, tile_step, 0)
    for r in range(8):
        rows = slice(r * 128, (r + 1) * 128)
        step = (acc_ref[rows, :128] + acc_ref[rows, 128:]).T
        out_ref[pl.ds(r, MEMBERS, stride=8), :] = x_ref[pl.ds(r, MEMBERS, stride=8), :] + step[:MEMBERS, :]


def update(bulk, at, tab, x, pos, own, side, off):
    def kernel(*refs):
        update_kernel(bulk, *refs)

    return pl.pallas_call(
        kernel,
        out_shape=jax.ShapeDtypeStruct((ROWS, 128), f32),
        in_specs=[SM, SM, VM, VM, VM, VM, VM],
        out_specs=VM,
        scratch_shapes=[
            pltpu.VMEM((CELLS, 256), bf16),
            pltpu.VMEM((TILES, 256, TILE), bf16),
            pltpu.VMEM((TILES, 256, TILE), bf16),
            pltpu.VMEM((TILES, 24, TILE), f32),
            pltpu.VMEM((CELLS, 256), f32),
            pltpu.VMEM((CELLS, 128), f32),
        ],
        compiler_params=PARAMS,
        cost_estimate=pl.CostEstimate(flops=6_000_000_000, bytes_accessed=2_000_000, transcendentals=0),
        name="update_cells" if bulk else "update_obs",
    )(at, tab, x, pos, own, side, off)


def unsend_kernel(x_ref, out_ref):
    for c in range(128):
        d, r = c // 8, c % 8
        out_ref[:, c * 128 : (c + 1) * 128] = x_ref[pl.ds(d * 40 + r, 5, stride=8), :]


def unsend(x):
    return pl.pallas_call(
        unsend_kernel,
        out_shape=jax.ShapeDtypeStruct((5, BLOCK), f32),
        in_specs=[VM],
        out_specs=VM,
        compiler_params=PARAMS,
        name="unsend",
    )(x)


def per_device(samples, quantity, variance, grid_point, sort, tab):
    count = lax.axis_size("space")
    space = lax.axis_index("space")
    member = lax.axis_index("member")
    swap = [(i, i ^ 1) for i in range(count)]
    hop = [(i, (i + (1 if i % 2 else -1)) % count) for i in range(count)]
    sign = jnp.where(space % 2 == 0, BLOCK, -BLOCK)
    at = jnp.stack([member * CELLS, sign, -sign]).astype(jnp.int32)
    par = jnp.stack([quantity, variance, grid_point.astype(f32), sort.astype(f32)], axis=1).reshape(2, 32, 128)

    send, picks = pick(samples, grid_point)
    gathered = lax.all_gather(picks, "member", axis=0).reshape(2 * ROWS, 128)
    cells = lax.all_to_all(send.reshape(16, 40, 128), "member", 0, 0, tiled=True).reshape(ROWS, 128)
    own, second = make_bundle(gathered, par[0])
    side = lax.ppermute(own, "space", swap)
    off = lax.ppermute(own, "space", hop)
    pos = par[1, 16:24]
    second = update(False, at, tab, second, pos, own, side, off)
    own2 = jnp.concatenate([second, par[1]], axis=0)
    side2 = lax.ppermute(own2, "space", swap)
    off2 = lax.ppermute(own2, "space", hop)
    cells = update(True, at, tab, cells, pos, own, side, off)
    cells = update(True, at, tab, cells, pos, own2, side2, off2)
    back = lax.all_to_all(cells.reshape(16, 5, 8, 128)
                          .reshape(ROWS, 128).reshape(16, 40, 128), "member", 0, 0, tiled=True)
    return unsend(back.reshape(ROWS, 128))


def solution(mesh):
    in_specs = (
        P("member", "space"),
        P(None, "space"),
        P(None, "space"),
        P(None, "space"),
        P(None, "space"),
        P(),
    )
    return jax.shard_map(
        per_device, mesh=mesh, in_specs=in_specs, out_specs=P("member", "space"), check_vma=False
    )
```

```python
import jax
import jax.numpy as jnp
from jax import lax
from jax.experimental import pallas as pl
from jax.experimental.pallas import tpu as pltpu
from jax.sharding import PartitionSpec as P

MEMBERS = 80
CELLS = 1024
BLOCK = 16384
BIN_BITS = 11
BINS = 8
CLASSES = 4
ROWS = 640
BUNDLE = 672
MERGED = 3072
f32 = jnp.float32
bf16 = jnp.bfloat16
VM = pl.BlockSpec(memory_space=pltpu.VMEM)
SM = pl.BlockSpec(memory_space=pltpu.SMEM)
PARAMS = pltpu.CompilerParams(vmem_limit_bytes=48 * 1024 * 1024)


def split(value):
    high = value.astype(bf16)
    low = (value - high.astype(f32)).astype(bf16)
    return high, low


def pick_kernel(
    x_hbm, value_hbm, error_hbm, gp_hbm, sort_hbm, send_ref, picks_ref, par_ref,
    x_ref, value_ref, error_ref, gp_ref, sort_ref, parts_ref, sems
):
    whole = ((x_hbm, x_ref), (gp_hbm, gp_ref), (value_hbm, value_ref), (error_hbm, error_ref), (sort_hbm, sort_ref))
    copies = [pltpu.make_async_copy(src, dst, sems.at[i]) for i, (src, dst) in enumerate(whole)]
    for copy in copies:
        copy.start()
    for copy in copies:
        copy.wait()
    for c in range(128):
        d, r = c // 8, c % 8
        slab = x_ref[:, c * 128 : (c + 1) * 128]
        send_ref[pl.ds(d * 40 + r, 5, stride=8), :] = slab
    for b in range(2):
        for at, ref in enumerate((value_ref, error_ref, gp_ref, sort_ref)):
            for r in range(8):
                row = ref[b : b + 1, r * 128 : (r + 1) * 128].astype(f32)
                par_ref[b * 32 + at * 8 + r : b * 32 + at * 8 + r + 1, :] = row
    lane = lax.broadcasted_iota(jnp.int32, (128, 128), 0)
    for m in range(5):
        slabs = jnp.concatenate([send_ref[d * 40 + m * 8 : d * 40 + m * 8 + 8, :] for d in range(16)], axis=0)
        high, low = split(slabs)
        parts_ref[m * 128 : (m + 1) * 128, :128] = high
        parts_ref[m * 128 : (m + 1) * 128, 128:] = low
    for b in range(2):
        for r in range(8):
            cell = gp_ref[b : b + 1, r * 128 : (r + 1) * 128]
            onehot = jnp.where((cell & 127) == lane, 1.0, 0.0).astype(bf16)
            found = jnp.dot(
                parts_ref[...], jnp.concatenate([onehot, onehot], axis=0), preferred_element_type=f32
            )
            here = lane == (cell >> 7)
            for m in range(5):
                value = jnp.where(here, found[m * 128 : (m + 1) * 128, :], 0.0)
                picks_ref[b * 40 + m * 8 + r : b * 40 + m * 8 + r + 1, :] = jnp.sum(value, axis=0, keepdims=True)


def pick(samples, quantity, variance, grid_point, sort):
    return pl.pallas_call(
        pick_kernel,
        out_shape=(
            jax.ShapeDtypeStruct((ROWS, 128), f32),
            jax.ShapeDtypeStruct((80, 128), f32),
            jax.ShapeDtypeStruct((64, 128), f32),
        ),
        in_specs=[pl.BlockSpec(memory_space=pltpu.HBM)] * 5,
        out_specs=(VM, VM, VM),
        scratch_shapes=[
            pltpu.VMEM(samples.shape, f32),
            pltpu.VMEM(quantity.shape, f32),
            pltpu.VMEM(variance.shape, f32),
            pltpu.VMEM(grid_point.shape, jnp.int32),
            pltpu.VMEM(sort.shape, jnp.int32),
            pltpu.VMEM((640, 256), bf16),
            pltpu.SemaphoreType.DMA((5,)),
        ],
        compiler_params=pltpu.CompilerParams(vmem_limit_bytes=63 * 1024 * 1024 + 512 * 1024),
        name="pick",
    )(samples, quantity, variance, grid_point, sort)


def bundle_kernel(gathered_ref, par_ref, bundle_ref, cells_ref):
    for k in range(16):
        bundle_ref[k * 40 : (k + 1) * 40, :] = gathered_ref[k * 80 : k * 80 + 40, :]
        cells_ref[k * 40 : (k + 1) * 40, :] = gathered_ref[k * 80 + 40 : k * 80 + 80, :]
    bundle_ref[ROWS:BUNDLE, :] = par_ref[...]


def make_bundle(gathered, par):
    return pl.pallas_call(
        bundle_kernel,
        out_shape=(jax.ShapeDtypeStruct((BUNDLE, 128), f32), jax.ShapeDtypeStruct((ROWS, 128), f32)),
        in_specs=[VM, VM],
        out_specs=(VM, VM),
        compiler_params=PARAMS,
        name="bundle",
    )(gathered, par)


def taper_of(classes, tab_ref):
    rows = []
    for b in range(BINS):
        row = jnp.zeros(classes.shape, f32)
        for c in range(CLASSES):
            row = jnp.where(classes == c, tab_ref[c, b], row)
        rows.append(row)
    return rows


def prepare_cells(x_ref, e3_ref):
    for r in range(8):
        cells = x_ref[pl.ds(r, MEMBERS, stride=8), :]
        dev = cells - jnp.sum(cells, axis=0, keepdims=True) / MEMBERS
        high = dev.astype(bf16).astype(f32)
        low = dev - high
        stacked = jnp.concatenate([high, low, high, jnp.zeros((16, 128), f32)], axis=0)
        e3_ref[r * 128 : (r + 1) * 128, :] = stacked.T.astype(bf16)


def prepare_section(sec, ref, tab_ref, d3_ref, a2_ref, rows_ref, start=None, shifted=None, place_ref=None):
    width = d3_ref.shape[2] // 128
    place = ref[656:664, :].astype(jnp.int32)
    classes = ref[664:672, :].astype(jnp.int32)
    taper = taper_of(classes, tab_ref)
    if shifted is None:
        first = start - place
        rising = first >= 0
        dist = jnp.abs(first)
        bin0 = dist >> BIN_BITS
        inner = dist & ((1 << BIN_BITS) - 1)
        turn = jnp.where(rising, (1 << BIN_BITS) - inner, inner + 1)
        bin1 = jnp.where(rising, bin0 + 1, jnp.maximum(bin0 - 1, 0))
        before = jnp.zeros(classes.shape, f32)
        after = jnp.zeros(classes.shape, f32)
        for b in range(BINS):
            before = jnp.where(bin0 == b, taper[b], before)
            after = jnp.where(bin1 == b, taper[b], after)
    else:
        shifted = shifted(place)
    for r in range(8):
        tile, col = (sec * 8 + r) // width, ((sec * 8 + r) % width) * 128
        cols = slice(col, col + 128)
        prior = ref[pl.ds(r, MEMBERS, stride=8), :]
        mean = jnp.sum(prior, axis=0, keepdims=True) / MEMBERS
        dev = prior - mean
        spread = jnp.sum(dev * dev, axis=0, keepdims=True) / (MEMBERS - 1)
        value = ref[640 + r : 641 + r, :]
        error = ref[648 + r : 649 + r, :]
        total = spread + error
        scale = 1.0 / (total * (MEMBERS - 1))
        shrink = 1.0 / (1.0 + jnp.sqrt(error / total))
        step = (value - mean) - shrink * dev
        high, low = split(dev)
        d3_ref[tile, 0:80, cols] = high
        d3_ref[tile, 80:160, cols] = high
        d3_ref[tile, 160:240, cols] = low
        d3_ref[tile, 240:256, cols] = jnp.zeros((16, 128), bf16)
        high, low = split(step)
        pad = jnp.zeros((48, 128), bf16)
        a2_ref[tile, 0:80, cols] = high
        a2_ref[tile, 80:128, cols] = pad
        a2_ref[tile, 128:208, cols] = low
        a2_ref[tile, 208:256, cols] = pad
        full = (8, 128)
        if shifted is None:
            rows_ref[tile, 0:8, cols] = jnp.broadcast_to(turn[r : r + 1, :].astype(f32), full)
            rows_ref[tile, 8:16, cols] = jnp.broadcast_to(before[r : r + 1, :] * scale, full)
            rows_ref[tile, 16:24, cols] = jnp.broadcast_to(after[r : r + 1, :] * scale, full)
        else:
            place_ref[tile, :, cols] = jnp.broadcast_to(shifted[r : r + 1, :], full)
            rows_ref[tile, :, cols] = jnp.concatenate([taper[b][r : r + 1, :] * scale for b in range(BINS)], axis=0)


def add_gains(rows, weight, cov, a2_ref, tile, acc_ref):
    gain = (weight * cov).reshape(cov.shape[0] * 8, cov.shape[2])
    high, low = split(gain)
    nt = (((1,), (1,)), ((), ()))
    acc_ref[rows, :] += lax.dot_general(high, a2_ref[tile], nt, preferred_element_type=f32)
    acc_ref[rows, :128] += lax.dot_general(low, a2_ref[tile, 0:128, :], nt, preferred_element_type=f32)


def scattered(tile, dist_of, masked, e3_ref, posb_ref, d3_ref, a2_ref, rows_ref, place_ref, acc_ref):
    part = 256
    width = d3_ref.shape[2]
    for ic in range(CELLS // part):
        rows = slice(ic * part, (ic + 1) * part)
        cov = jnp.dot(e3_ref[rows, :], d3_ref[tile], preferred_element_type=f32).reshape(part // 8, 8, width)
        groups = []
        for h in range(width // 128):
            cols = slice(h * 128, (h + 1) * 128)
            place = place_ref[tile, :, cols]
            table = rows_ref[tile, :, cols]
            slabs = []
            for g in range(part // 8):
                at = ic * part + g * 8
                level = dist_of(posb_ref[at : at + 8, :], place) >> BIN_BITS
                if masked:
                    got = jnp.take_along_axis(table, level & (BINS - 1), axis=0, mode="promise_in_bounds")
                    got = jnp.where(level < BINS, got, 0.0)
                else:
                    got = jnp.take_along_axis(table, level, axis=0, mode="promise_in_bounds")
                slabs.append(got[None])
            groups.append(jnp.concatenate(slabs, axis=0))
        add_gains(rows, jnp.concatenate(groups, axis=2), cov, a2_ref, tile, acc_ref)


def place_cells(pos_ref, posb_ref, sign):
    for r in range(8):
        row = jnp.broadcast_to(pos_ref[r : r + 1, :], (128, 128))
        posb_ref[r * 128 : (r + 1) * 128, :] = row.T.astype(jnp.int32) * sign


def replay_chip_kernel(
    at_ref, tab_ref, x_ref, pos_ref, own_ref, side_ref, out_ref,
    e3_ref, posb_ref, acc_ref, d3_ref, a2_ref, rows_ref, place_ref
):
    sign = at_ref[1]
    prepare_cells(x_ref, e3_ref)
    place_cells(pos_ref, posb_ref, sign)
    work = (e3_ref, posb_ref, d3_ref, a2_ref, rows_ref, place_ref, acc_ref)
    prepare_section(
        0, own_ref, tab_ref, d3_ref, a2_ref, rows_ref, shifted=lambda place: place * sign, place_ref=place_ref
    )
    prepare_section(
        1, side_ref.at[at_ref[2]], tab_ref, d3_ref, a2_ref, rows_ref,
        shifted=lambda place: place * sign + BLOCK, place_ref=place_ref,
    )
    acc_ref[...] = jnp.zeros_like(acc_ref)
    scattered(0, lambda pos, place: jnp.abs(pos - place), False, *work)
    scattered(1, lambda pos, place: place - pos, True, *work)
    finish(x_ref, acc_ref, out_ref)


def replay_off_kernel(
    at_ref, tab_ref, x_ref, pos_ref, part_ref, off_ref, par_ref, out_ref,
    e3_ref, posb_ref, acc_ref, d3_ref, a2_ref, rows_ref, place_ref
):
    sign = at_ref[1]
    prepare_cells(x_ref, e3_ref)
    place_cells(pos_ref, posb_ref, sign)
    work = (e3_ref, posb_ref, d3_ref, a2_ref, rows_ref, place_ref, acc_ref)
    prepare_section(
        0, off_ref, tab_ref, d3_ref, a2_ref, rows_ref,
        shifted=lambda place: place * sign - BLOCK, place_ref=place_ref,
    )
    acc_ref[...] = jnp.zeros_like(acc_ref)
    scattered(0, lambda pos, place: pos - place, True, *work)
    finish(part_ref, acc_ref, out_ref)
    out_ref[ROWS:BUNDLE, :] = par_ref[...]


def replay(kernel, sections, rows, name, at, tab, *arrays):
    return pl.pallas_call(
        kernel,
        out_shape=jax.ShapeDtypeStruct((rows, 128), f32),
        in_specs=[SM, SM] + [VM] * len(arrays),
        out_specs=VM,
        scratch_shapes=[
            pltpu.VMEM((CELLS, 256), bf16),
            pltpu.VMEM((CELLS, 128), jnp.int32),
            pltpu.VMEM((CELLS, 256), f32),
            pltpu.VMEM((sections, 256, 1024), bf16),
            pltpu.VMEM((sections, 256, 1024), bf16),
            pltpu.VMEM((sections, 8, 1024), f32),
            pltpu.VMEM((sections, 8, 1024), jnp.int32),
        ],
        compiler_params=PARAMS,
        cost_estimate=pl.CostEstimate(flops=4_000_000_000 * sections, bytes_accessed=2_000_000, transcendentals=0),
        name=name,
    )(at, tab, *arrays)


def finish(x_ref, acc_ref, out_ref):
    for r in range(8):
        rows = slice(r * 128, (r + 1) * 128)
        step = (acc_ref[rows, :128] + acc_ref[rows, 128:]).T
        out_ref[pl.ds(r, MEMBERS, stride=8), :] = x_ref[pl.ds(r, MEMBERS, stride=8), :] + step[:MEMBERS, :]


def update_kernel(at_ref, tab_ref, x_ref, own_ref, side_ref, off_ref, out_ref, e3_ref, d3_ref, a2_ref, rows_ref, acc_ref):
    start, sign = at_ref[0], at_ref[1]
    prepare_cells(x_ref, e3_ref)
    sections = ((own_ref, start), (side_ref.at[at_ref[2]], start - sign * BLOCK), (off_ref, start + sign * BLOCK))
    for sec, (ref, first) in enumerate(sections):
        prepare_section(sec, ref, tab_ref, d3_ref, a2_ref, rows_ref, start=first)
    acc_ref[...] = jnp.zeros_like(acc_ref)
    tiles, _, width = d3_ref.shape
    part = CELLS

    def tile_step(tile, carry):
        for ic in range(CELLS // part):
            rows = slice(ic * part, (ic + 1) * part)
            shape = (part // 8, 8, width)
            cov = jnp.dot(e3_ref[rows, :], d3_ref[tile], preferred_element_type=f32).reshape(shape)
            at = lax.broadcasted_iota(jnp.int32, (part, width), 0).astype(f32).reshape(shape) + float(ic * part)
            turn = rows_ref[tile, 0:8, :][None]
            weight = jnp.where(at >= turn, rows_ref[tile, 16:24, :][None], rows_ref[tile, 8:16, :][None])
            add_gains(rows, weight, cov, a2_ref, tile, acc_ref)
        return carry

    lax.fori_loop(0, tiles, tile_step, 0, unroll=2)
    finish(x_ref, acc_ref, out_ref)


def update(at, tab, x, own, side, off):
    width = 512
    tiles = MERGED // width
    return pl.pallas_call(
        update_kernel,
        out_shape=jax.ShapeDtypeStruct((ROWS, 128), f32),
        in_specs=[SM, SM, VM, VM, VM, VM],
        out_specs=VM,
        scratch_shapes=[
            pltpu.VMEM((CELLS, 256), bf16),
            pltpu.VMEM((tiles, 256, width), bf16),
            pltpu.VMEM((tiles, 256, width), bf16),
            pltpu.VMEM((tiles, 24, width), f32),
            pltpu.VMEM((CELLS, 256), f32),
        ],
        compiler_params=PARAMS,
        cost_estimate=pl.CostEstimate(flops=9_000_000_000, bytes_accessed=2_000_000, transcendentals=0),
        name="update_cells",
    )(at, tab, x, own, side, off)


def unsend_kernel(x_ref, out_ref):
    for c in range(128):
        d, r = c // 8, c % 8
        out_ref[:, c * 128 : (c + 1) * 128] = x_ref[pl.ds(d * 40 + r, 5, stride=8), :]


def unsend(x):
    return pl.pallas_call(
        unsend_kernel,
        out_shape=jax.ShapeDtypeStruct((5, BLOCK), f32),
        in_specs=[VM],
        out_specs=VM,
        compiler_params=PARAMS,
        name="unsend",
    )(x)


def per_device(samples, quantity, variance, grid_point, sort, tab):
    count = lax.axis_size("space")
    space = lax.axis_index("space")
    member = lax.axis_index("member")
    pairs = [[i, i + 1] for i in range(0, count, 2)]
    hop = [(i, (i + (1 if i % 2 else -1)) % count) for i in range(count)]
    odd = space % 2
    at = jnp.stack([member * CELLS, 1 - 2 * odd, 1 - odd]).astype(jnp.int32)

    send, picks, par = pick(samples, quantity, variance, grid_point, sort)
    par = par.reshape(2, 32, 128)
    gathered = lax.all_gather(picks, "member", axis=0).reshape(2 * ROWS, 128)
    own, second = make_bundle(gathered, par[0])
    send, own = lax.optimization_barrier((send, own))
    cells = lax.all_to_all(send.reshape(16, 40, 128), "member", 0, 0, tiled=True).reshape(ROWS, 128)
    off = lax.ppermute(own, "space", hop)
    side = lax.all_gather(own, "space", axis_index_groups=pairs)
    pos = par[1, 16:24]
    part = replay(replay_chip_kernel, 2, ROWS, "replay_chip", at, tab, second, pos, own, side)
    own2 = replay(replay_off_kernel, 1, BUNDLE, "replay_off", at, tab, second, pos, part, off, par[1])
    off2 = lax.ppermute(own2, "space", hop)
    side2 = lax.all_gather(own2, "space", axis_index_groups=pairs)
    cells = update(at, tab, cells, own, side, off)
    cells = update(at, tab, cells, own2, side2, off2)
    back = lax.all_to_all(cells.reshape(16, 40, 128), "member", 0, 0, tiled=True)
    return unsend(back.reshape(ROWS, 128))


def solution(mesh):
    in_specs = (
        P("member", "space"),
        P(None, "space"),
        P(None, "space"),
        P(None, "space"),
        P(None, "space"),
        P(),
    )
    return jax.shard_map(
        per_device, mesh=mesh, in_specs=in_specs, out_specs=P("member", "space"), check_vma=False
    )
```

```python
import jax
import jax.numpy as jnp
from jax import lax
from jax.experimental import pallas as pl
from jax.experimental.pallas import tpu as pltpu
from jax.sharding import PartitionSpec as P

MEMBERS = 80
CELLS = 1024
BLOCK = 16384
BIN_BITS = 11
BINS = 8
CLASSES = 4
ROWS = 640
BUNDLE = 96
VALUE, ERROR, PLACE, KIND, TABLE = 80, 81, 82, 83, 88
MERGED = 3072
CHUNKS = 4
PICK_VMEM = 62 * 1024 * 1024 + 768 * 1024
f32 = jnp.float32
bf16 = jnp.bfloat16
VM = pl.BlockSpec(memory_space=pltpu.VMEM)
SM = pl.BlockSpec(memory_space=pltpu.SMEM)
PARAMS = pltpu.CompilerParams(vmem_limit_bytes=48 * 1024 * 1024)


def split(value):
    high = value.astype(bf16)
    low = (value - high.astype(f32)).astype(bf16)
    return high, low


def pick_kernel(
    x_hbm, value_hbm, error_hbm, gp_hbm, sort_hbm, tab_hbm, send_ref, picks_ref, par_ref,
    x_ref, value_ref, error_ref, gp_ref, sort_ref, tab_ref, parts_ref, sems
):
    small = ((value_hbm, value_ref), (error_hbm, error_ref), (gp_hbm, gp_ref), (sort_hbm, sort_ref), (tab_hbm, tab_ref))
    copies = []
    for i in range(CHUNKS):
        cols = pl.ds(i * (BLOCK // CHUNKS), BLOCK // CHUNKS)
        copies.append(pltpu.make_async_copy(x_hbm.at[:, cols], x_ref.at[:, cols], sems.at[i]))
    for i, (src, dst) in enumerate(small):
        copies.append(pltpu.make_async_copy(src, dst, sems.at[CHUNKS + i]))
    for copy in copies[CHUNKS:] + copies[:CHUNKS]:
        copy.start()
    for copy in copies[CHUNKS:]:
        copy.wait()
    for b in range(2):
        for at, ref in enumerate((value_ref, error_ref, gp_ref, sort_ref)):
            par_ref[b * 16 + at : b * 16 + at + 1, :] = ref[b : b + 1, :].astype(f32)
        par_ref[b * 16 + 4 : b * 16 + 8, :] = jnp.zeros((4, CELLS), f32)
        kind = sort_ref[b : b + 1, :]
        for level in range(BINS):
            row = jnp.zeros((1, CELLS), f32)
            for c in range(CLASSES):
                row = jnp.where(kind == c, tab_ref[c : c + 1, level : level + 1], row)
            par_ref[b * 16 + 8 + level : b * 16 + 9 + level, :] = row
    each = 16 // CHUNKS
    for i in range(CHUNKS):
        copies[i].wait()
        for c in range(i * 8 * each, (i + 1) * 8 * each):
            d, r = c // 8, c % 8
            send_ref[pl.ds(d * 40 + r, 5, stride=8), :] = x_ref[:, c * 128 : (c + 1) * 128]
        for m in range(5):
            begin = i * each * 40 + m * 8
            slabs = jnp.concatenate([send_ref[begin + d * 40 : begin + d * 40 + 8, :] for d in range(each)], axis=0)
            high, low = split(slabs)
            rows = slice(m * 128 + i * each * 8, m * 128 + (i + 1) * each * 8)
            parts_ref[rows, :128] = high
            parts_ref[rows, 128:] = low
    lane = lax.broadcasted_iota(jnp.int32, (128, 256), 0)
    for b in range(2):
        for h in range(4):
            cell = gp_ref[b : b + 1, h * 256 : (h + 1) * 256]
            onehot = jnp.where((cell & 127) == lane, 1.0, 0.0).astype(bf16)
            found = jnp.dot(
                parts_ref[...], jnp.concatenate([onehot, onehot], axis=0), preferred_element_type=f32
            )
            here = lane == (cell >> 7)
            for m in range(5):
                value = jnp.where(here, found[m * 128 : (m + 1) * 128, :], 0.0)
                value = jnp.sum(value, axis=0, keepdims=True)
                row = b * 40 + m * 8 + h * 2
                picks_ref[row : row + 1, :] = value[:, :128]
                picks_ref[row + 1 : row + 2, :] = value[:, 128:]


def pick(samples, quantity, variance, grid_point, sort, tab):
    return pl.pallas_call(
        pick_kernel,
        out_shape=(
            jax.ShapeDtypeStruct((ROWS, 128), f32),
            jax.ShapeDtypeStruct((80, 128), f32),
            jax.ShapeDtypeStruct((32, CELLS), f32),
        ),
        in_specs=[pl.BlockSpec(memory_space=pltpu.HBM)] * 6,
        out_specs=(VM, VM, VM),
        scratch_shapes=[
            pltpu.VMEM(samples.shape, f32),
            pltpu.VMEM(quantity.shape, f32),
            pltpu.VMEM(variance.shape, f32),
            pltpu.VMEM(grid_point.shape, jnp.int32),
            pltpu.VMEM(sort.shape, jnp.int32),
            pltpu.VMEM(tab.shape, f32),
            pltpu.VMEM((640, 256), bf16),
            pltpu.SemaphoreType.DMA((CHUNKS + 5,)),
        ],
        compiler_params=pltpu.CompilerParams(vmem_limit_bytes=PICK_VMEM),
        name="pick",
    )(samples, quantity, variance, grid_point, sort, tab)


def bundle_kernel(gathered_ref, par_ref, bundle_ref, cells_ref, first_ref, second_ref):
    for k in range(16):
        first_ref[k * 40 : (k + 1) * 40, :] = gathered_ref[k * 80 : k * 80 + 40, :]
        second_ref[k * 40 : (k + 1) * 40, :] = gathered_ref[k * 80 + 40 : k * 80 + 80, :]
    for r in range(8):
        cols = slice(r * 128, (r + 1) * 128)
        bundle_ref[0:MEMBERS, cols] = first_ref[pl.ds(r, MEMBERS, stride=8), :]
        cells_ref[:, cols] = second_ref[pl.ds(r, MEMBERS, stride=8), :]
    bundle_ref[MEMBERS:BUNDLE, :] = par_ref[0:16, :]


def make_bundle(gathered, par):
    return pl.pallas_call(
        bundle_kernel,
        out_shape=(jax.ShapeDtypeStruct((BUNDLE, CELLS), f32), jax.ShapeDtypeStruct((MEMBERS, CELLS), f32)),
        in_specs=[VM, VM],
        out_specs=(VM, VM),
        scratch_shapes=[pltpu.VMEM((ROWS, 128), f32), pltpu.VMEM((ROWS, 128), f32)],
        compiler_params=PARAMS,
        name="bundle",
    )(gathered, par)


def prepare_cells(x_ref, e3_ref):
    for r in range(8):
        cells = x_ref[:, r * 128 : (r + 1) * 128]
        dev = cells - jnp.sum(cells, axis=0, keepdims=True) / MEMBERS
        high = dev.astype(bf16).astype(f32)
        low = dev - high
        stacked = jnp.concatenate([high, low, high, jnp.zeros((16, 128), f32)], axis=0)
        e3_ref[r * 128 : (r + 1) * 128, :] = stacked.T.astype(bf16)


def prepare_section(sec, ref, d3_ref, a2_ref, rows_ref, start=None, shifted=None, place_ref=None):
    width = d3_ref.shape[2] // 128
    for r in range(8):
        tile, col = (sec * 8 + r) // width, ((sec * 8 + r) % width) * 128
        cols = slice(col, col + 128)
        here = slice(r * 128, (r + 1) * 128)
        prior = ref[0:MEMBERS, here]
        mean = jnp.sum(prior, axis=0, keepdims=True) / MEMBERS
        dev = prior - mean
        spread = jnp.sum(dev * dev, axis=0, keepdims=True) / (MEMBERS - 1)
        value = ref[VALUE : VALUE + 1, here]
        error = ref[ERROR : ERROR + 1, here]
        place = ref[PLACE : PLACE + 1, here].astype(jnp.int32)
        total = spread + error
        scale = 1.0 / (total * (MEMBERS - 1))
        shrink = 1.0 / (1.0 + jnp.sqrt(error / total))
        step = (value - mean) - shrink * dev
        high, low = split(dev)
        d3_ref[tile, 0:80, cols] = high
        d3_ref[tile, 80:160, cols] = high
        d3_ref[tile, 160:240, cols] = low
        d3_ref[tile, 240:256, cols] = jnp.zeros((16, 128), bf16)
        high, low = split(step)
        pad = jnp.zeros((48, 128), bf16)
        a2_ref[tile, 0:80, cols] = high
        a2_ref[tile, 80:128, cols] = pad
        a2_ref[tile, 128:208, cols] = low
        a2_ref[tile, 208:256, cols] = pad
        full = (8, 128)
        table = ref[TABLE : TABLE + BINS, here] * scale
        if shifted is None:
            first = start - place
            rising = first >= 0
            dist = jnp.abs(first)
            bin0 = dist >> BIN_BITS
            inner = dist & ((1 << BIN_BITS) - 1)
            turn = jnp.where(rising, (1 << BIN_BITS) - inner, inner + 1)
            bin1 = jnp.where(rising, bin0 + 1, jnp.maximum(bin0 - 1, 0))
            level = lax.broadcasted_iota(jnp.int32, full, 0)
            before = jnp.sum(jnp.where(level == bin0, table, 0.0), axis=0, keepdims=True)
            after = jnp.sum(jnp.where(level == bin1, table, 0.0), axis=0, keepdims=True)
            rows_ref[tile, 0:8, cols] = jnp.broadcast_to(turn.astype(f32), full)
            rows_ref[tile, 8:16, cols] = jnp.broadcast_to(before, full)
            rows_ref[tile, 16:24, cols] = jnp.broadcast_to(after, full)
        else:
            place_ref[tile, :, cols] = jnp.broadcast_to(shifted(place), full)
            rows_ref[tile, :, cols] = table


def add_gains(rows, weight, cov, a2_ref, tile, acc_ref):
    gain = (weight * cov).reshape(cov.shape[0] * 8, cov.shape[2])
    high, low = split(gain)
    nt = (((1,), (1,)), ((), ()))
    acc_ref[rows, :] += lax.dot_general(high, a2_ref[tile], nt, preferred_element_type=f32)
    acc_ref[rows, :128] += lax.dot_general(low, a2_ref[tile, 0:128, :], nt, preferred_element_type=f32)


def scattered(tile, dist_of, masked, e3_ref, posb_ref, d3_ref, a2_ref, rows_ref, place_ref, acc_ref):
    part = 256
    width = d3_ref.shape[2]
    for ic in range(CELLS // part):
        rows = slice(ic * part, (ic + 1) * part)
        cov = jnp.dot(e3_ref[rows, :], d3_ref[tile], preferred_element_type=f32).reshape(part // 8, 8, width)
        groups = []
        for h in range(width // 128):
            cols = slice(h * 128, (h + 1) * 128)
            place = place_ref[tile, :, cols]
            table = rows_ref[tile, :, cols]
            slabs = []
            for g in range(part // 8):
                at = ic * part + g * 8
                level = dist_of(posb_ref[at : at + 8, :], place) >> BIN_BITS
                if masked:
                    got = jnp.take_along_axis(table, level & (BINS - 1), axis=0, mode="promise_in_bounds")
                    got = jnp.where(level < BINS, got, 0.0)
                else:
                    got = jnp.take_along_axis(table, level, axis=0, mode="promise_in_bounds")
                slabs.append(got[None])
            groups.append(jnp.concatenate(slabs, axis=0))
        add_gains(rows, jnp.concatenate(groups, axis=2), cov, a2_ref, tile, acc_ref)


def place_cells(par_ref, posb_ref, sign):
    for r in range(8):
        row = jnp.broadcast_to(par_ref[18:19, r * 128 : (r + 1) * 128], (128, 128))
        posb_ref[r * 128 : (r + 1) * 128, :] = row.T.astype(jnp.int32) * sign


def replay_kernel(
    at_ref, par_ref, x_ref, own_ref, side_ref, off_ref, out_ref,
    e3_ref, posb_ref, acc_ref, d3_ref, a2_ref, rows_ref, place_ref
):
    sign = at_ref[1]
    prepare_cells(x_ref, e3_ref)
    place_cells(par_ref, posb_ref, sign)
    work = (e3_ref, posb_ref, d3_ref, a2_ref, rows_ref, place_ref, acc_ref)
    sections = (
        (own_ref, lambda place: place * sign),
        (side_ref.at[at_ref[2]], lambda place: place * sign + BLOCK),
        (off_ref, lambda place: place * sign - BLOCK),
    )
    for sec, (ref, shifted) in enumerate(sections):
        prepare_section(sec, ref, d3_ref, a2_ref, rows_ref, shifted=shifted, place_ref=place_ref)
    acc_ref[...] = jnp.zeros_like(acc_ref)
    scattered(0, lambda pos, place: jnp.abs(pos - place), False, *work)
    scattered(1, lambda pos, place: place - pos, True, *work)
    scattered(2, lambda pos, place: pos - place, True, *work)
    finish(x_ref, acc_ref, out_ref)
    out_ref[MEMBERS:BUNDLE, :] = par_ref[16:32, :]


def replay(kernel, sections, name, at, par, *arrays):
    return pl.pallas_call(
        kernel,
        out_shape=jax.ShapeDtypeStruct((BUNDLE, CELLS), f32),
        in_specs=[SM, VM] + [VM] * len(arrays),
        out_specs=VM,
        scratch_shapes=[
            pltpu.VMEM((CELLS, 256), bf16),
            pltpu.VMEM((CELLS, 128), jnp.int32),
            pltpu.VMEM((CELLS, 256), f32),
            pltpu.VMEM((sections, 256, 1024), bf16),
            pltpu.VMEM((sections, 256, 1024), bf16),
            pltpu.VMEM((sections, 8, 1024), f32),
            pltpu.VMEM((sections, 8, 1024), jnp.int32),
        ],
        compiler_params=PARAMS,
        cost_estimate=pl.CostEstimate(flops=4_000_000_000 * sections, bytes_accessed=2_000_000, transcendentals=0),
        name=name,
    )(at, par, *arrays)


def finish(x_ref, acc_ref, out_ref, strided=False):
    for r in range(8):
        rows = slice(r * 128, (r + 1) * 128)
        step = (acc_ref[rows, :128] + acc_ref[rows, 128:]).T
        value = x_ref[:, rows] + step[:MEMBERS, :]
        if strided:
            out_ref[pl.ds(r, MEMBERS, stride=8), :] = value
        else:
            out_ref[0:MEMBERS, rows] = value


def update_kernel(
    last, at_ref, cells_ref, own_ref, side_ref, off_ref, out_ref, x_ref, e3_ref, d3_ref, a2_ref, rows_ref, acc_ref
):
    start, sign = at_ref[0], at_ref[1]
    if last:
        x_ref = cells_ref
    else:
        for r in range(8):
            x_ref[:, r * 128 : (r + 1) * 128] = cells_ref[pl.ds(r, MEMBERS, stride=8), :]
    prepare_cells(x_ref, e3_ref)
    sections = ((own_ref, start), (side_ref.at[0 if last else at_ref[2]], start - sign * BLOCK), (off_ref, start + sign * BLOCK))
    for sec, (ref, first) in enumerate(sections):
        prepare_section(sec, ref, d3_ref, a2_ref, rows_ref, start=first)
    acc_ref[...] = jnp.zeros_like(acc_ref)
    tiles, _, width = d3_ref.shape
    part = CELLS

    def tile_step(tile, carry):
        for ic in range(CELLS // part):
            rows = slice(ic * part, (ic + 1) * part)
            shape = (part // 8, 8, width)
            cov = jnp.dot(e3_ref[rows, :], d3_ref[tile], preferred_element_type=f32).reshape(shape)
            at = lax.broadcasted_iota(jnp.int32, (part, width), 0).astype(f32).reshape(shape) + float(ic * part)
            turn = rows_ref[tile, 0:8, :][None]
            weight = jnp.where(at >= turn, rows_ref[tile, 16:24, :][None], rows_ref[tile, 8:16, :][None])
            add_gains(rows, weight, cov, a2_ref, tile, acc_ref)
        return carry

    lax.fori_loop(0, tiles, tile_step, 0, unroll=tiles)
    finish(x_ref, acc_ref, out_ref, strided=last)


def update(last, at, x, own, side, off):
    def kernel(*refs):
        update_kernel(last, *refs)

    width = 768
    tiles = MERGED // width
    return pl.pallas_call(
        kernel,
        out_shape=jax.ShapeDtypeStruct((ROWS, 128) if last else (MEMBERS, CELLS), f32),
        in_specs=[SM, VM, VM, VM, VM],
        out_specs=VM,
        scratch_shapes=[
            pltpu.VMEM((MEMBERS, CELLS), f32),
            pltpu.VMEM((CELLS, 256), bf16),
            pltpu.VMEM((tiles, 256, width), bf16),
            pltpu.VMEM((tiles, 256, width), bf16),
            pltpu.VMEM((tiles, 24, width), f32),
            pltpu.VMEM((CELLS, 256), f32),
        ],
        compiler_params=PARAMS,
        cost_estimate=pl.CostEstimate(flops=9_000_000_000, bytes_accessed=2_000_000, transcendentals=0),
        name="update_last" if last else "update_first",
    )(at, x, own, side, off)


def unsend_kernel(x_ref, out_ref):
    for c in range(128):
        d, r = c // 8, c % 8
        out_ref[:, c * 128 : (c + 1) * 128] = x_ref[pl.ds(d * 40 + r, 5, stride=8), :]


def unsend(x):
    return pl.pallas_call(
        unsend_kernel,
        out_shape=jax.ShapeDtypeStruct((5, BLOCK), f32),
        in_specs=[VM],
        out_specs=VM,
        compiler_params=PARAMS,
        name="unsend",
    )(x)


def per_device(samples, quantity, variance, grid_point, sort, tab):
    count = lax.axis_size("space")
    space = lax.axis_index("space")
    member = lax.axis_index("member")
    pairs = [[i, i + 1] for i in range(0, count, 2)]
    swap = [(i, i ^ 1) for i in range(count)]
    hop = [(i, (i + (1 if i % 2 else -1)) % count) for i in range(count)]
    odd = space % 2
    at = jnp.stack([member * CELLS, 1 - 2 * odd, 1 - odd]).astype(jnp.int32)

    send, picks, par = pick(samples, quantity, variance, grid_point, sort, tab)
    gathered = lax.all_gather(picks, "member", axis=0).reshape(2 * ROWS, 128)
    own, second = make_bundle(gathered, par)
    off = lax.ppermute(own, "space", hop)
    side = lax.all_gather(own, "space", axis_index_groups=pairs)
    send, side = lax.optimization_barrier((send, side))
    cells = lax.all_to_all(send.reshape(16, 40, 128), "member", 0, 0, tiled=True).reshape(ROWS, 128)
    own2 = replay(replay_kernel, 3, "replay", at, par, second, own, side, off)
    off2 = lax.ppermute(own2, "space", hop)
    side2 = lax.ppermute(own2, "space", swap)[None]
    cells = update(False, at, cells, own, side, off)
    cells = update(True, at, cells, own2, side2, off2)
    back = lax.all_to_all(cells.reshape(16, 40, 128), "member", 0, 0, tiled=True)
    return unsend(back.reshape(ROWS, 128))


def solution(mesh):
    in_specs = (
        P("member", "space"),
        P(None, "space"),
        P(None, "space"),
        P(None, "space"),
        P(None, "space"),
        P(),
    )
    return jax.shard_map(
        per_device, mesh=mesh, in_specs=in_specs, out_specs=P("member", "space"), check_vma=False
    )
```

```python
import jax
import jax.numpy as jnp
from jax import lax
from jax.experimental import pallas as pl
from jax.experimental.pallas import tpu as pltpu
from jax.sharding import PartitionSpec as P

MEMBERS = 80
CELLS = 1024
BLOCK = 16384
BIN_BITS = 11
BINS = 8
CLASSES = 4
ROWS = 640
BUNDLE = 96
VALUE, ERROR, PLACE, KIND, TABLE = 80, 81, 82, 83, 88
MERGED = 3072
CHUNKS = 4
PICK_VMEM = 62 * 1024 * 1024 + 768 * 1024
f32 = jnp.float32
bf16 = jnp.bfloat16
VM = pl.BlockSpec(memory_space=pltpu.VMEM)
SM = pl.BlockSpec(memory_space=pltpu.SMEM)
PARAMS = pltpu.CompilerParams(vmem_limit_bytes=48 * 1024 * 1024)


def split(value):
    high = value.astype(bf16)
    low = (value - high.astype(f32)).astype(bf16)
    return high, low


def pick_kernel(
    x_hbm, value_hbm, error_hbm, gp_hbm, sort_hbm, tab_hbm, send_ref, picks_ref, par_ref,
    x_ref, value_ref, error_ref, gp_ref, sort_ref, tab_ref, parts_ref, sems
):
    small = ((value_hbm, value_ref), (error_hbm, error_ref), (gp_hbm, gp_ref), (sort_hbm, sort_ref), (tab_hbm, tab_ref))
    copies = []
    for i in range(CHUNKS):
        cols = pl.ds(i * (BLOCK // CHUNKS), BLOCK // CHUNKS)
        copies.append(pltpu.make_async_copy(x_hbm.at[:, cols], x_ref.at[:, cols], sems.at[i]))
    for i, (src, dst) in enumerate(small):
        copies.append(pltpu.make_async_copy(src, dst, sems.at[CHUNKS + i]))
    for copy in copies[CHUNKS:] + copies[:CHUNKS]:
        copy.start()
    for copy in copies[CHUNKS:]:
        copy.wait()
    for b in range(2):
        for at, ref in enumerate((value_ref, error_ref, gp_ref, sort_ref)):
            par_ref[b * 16 + at : b * 16 + at + 1, :] = ref[b : b + 1, :].astype(f32)
        par_ref[b * 16 + 4 : b * 16 + 8, :] = jnp.zeros((4, CELLS), f32)
        kind = sort_ref[b : b + 1, :]
        for level in range(BINS):
            row = jnp.zeros((1, CELLS), f32)
            for c in range(CLASSES):
                row = jnp.where(kind == c, tab_ref[c : c + 1, level : level + 1], row)
            par_ref[b * 16 + 8 + level : b * 16 + 9 + level, :] = row
    each = 16 // CHUNKS
    for i in range(CHUNKS):
        copies[i].wait()
        for c in range(i * 8 * each, (i + 1) * 8 * each):
            d, r = c // 8, c % 8
            send_ref[pl.ds(d * 40 + r, 5, stride=8), :] = x_ref[:, c * 128 : (c + 1) * 128]
        for m in range(5):
            begin = i * each * 40 + m * 8
            slabs = jnp.concatenate([send_ref[begin + d * 40 : begin + d * 40 + 8, :] for d in range(each)], axis=0)
            high, low = split(slabs)
            rows = slice(m * 128 + i * each * 8, m * 128 + (i + 1) * each * 8)
            parts_ref[rows, :128] = high
            parts_ref[rows, 128:] = low
    lane = lax.broadcasted_iota(jnp.int32, (128, 256), 0)
    for b in range(2):
        for h in range(4):
            cell = gp_ref[b : b + 1, h * 256 : (h + 1) * 256]
            onehot = jnp.where((cell & 127) == lane, 1.0, 0.0).astype(bf16)
            found = jnp.dot(
                parts_ref[...], jnp.concatenate([onehot, onehot], axis=0), preferred_element_type=f32
            )
            here = lane == (cell >> 7)
            for m in range(5):
                value = jnp.where(here, found[m * 128 : (m + 1) * 128, :], 0.0)
                value = jnp.sum(value, axis=0, keepdims=True)
                row = b * 40 + m * 8 + h * 2
                picks_ref[row : row + 1, :] = value[:, :128]
                picks_ref[row + 1 : row + 2, :] = value[:, 128:]


def pick(samples, quantity, variance, grid_point, sort, tab):
    return pl.pallas_call(
        pick_kernel,
        out_shape=(
            jax.ShapeDtypeStruct((ROWS, 128), f32),
            jax.ShapeDtypeStruct((80, 128), f32),
            jax.ShapeDtypeStruct((32, CELLS), f32),
        ),
        in_specs=[pl.BlockSpec(memory_space=pltpu.HBM)] * 6,
        out_specs=(VM, VM, VM),
        scratch_shapes=[
            pltpu.VMEM(samples.shape, f32),
            pltpu.VMEM(quantity.shape, f32),
            pltpu.VMEM(variance.shape, f32),
            pltpu.VMEM(grid_point.shape, jnp.int32),
            pltpu.VMEM(sort.shape, jnp.int32),
            pltpu.VMEM(tab.shape, f32),
            pltpu.VMEM((640, 256), bf16),
            pltpu.SemaphoreType.DMA((CHUNKS + 5,)),
        ],
        compiler_params=pltpu.CompilerParams(vmem_limit_bytes=PICK_VMEM),
        name="pick",
    )(samples, quantity, variance, grid_point, sort, tab)


def bundle_kernel(gathered_ref, par_ref, bundle_ref, cells_ref, first_ref, second_ref):
    for k in range(16):
        first_ref[k * 40 : (k + 1) * 40, :] = gathered_ref[k * 80 : k * 80 + 40, :]
        second_ref[k * 40 : (k + 1) * 40, :] = gathered_ref[k * 80 + 40 : k * 80 + 80, :]
    for r in range(8):
        cols = slice(r * 128, (r + 1) * 128)
        bundle_ref[0:MEMBERS, cols] = first_ref[pl.ds(r, MEMBERS, stride=8), :]
        cells_ref[:, cols] = second_ref[pl.ds(r, MEMBERS, stride=8), :]
    bundle_ref[MEMBERS:BUNDLE, :] = par_ref[0:16, :]


def make_bundle(gathered, par):
    return pl.pallas_call(
        bundle_kernel,
        out_shape=(jax.ShapeDtypeStruct((BUNDLE, CELLS), f32), jax.ShapeDtypeStruct((MEMBERS, CELLS), f32)),
        in_specs=[VM, VM],
        out_specs=(VM, VM),
        scratch_shapes=[pltpu.VMEM((ROWS, 128), f32), pltpu.VMEM((ROWS, 128), f32)],
        compiler_params=PARAMS,
        name="bundle",
    )(gathered, par)


def prepare_cells(x_ref, e3_ref):
    for r in range(8):
        cells = x_ref[:, r * 128 : (r + 1) * 128]
        dev = cells - jnp.sum(cells, axis=0, keepdims=True) / MEMBERS
        high = dev.astype(bf16).astype(f32)
        low = dev - high
        stacked = jnp.concatenate([high, low, high, jnp.zeros((16, 128), f32)], axis=0)
        e3_ref[r * 128 : (r + 1) * 128, :] = stacked.T.astype(bf16)


def prepare_section(sec, ref, d3_ref, a2_ref, rows_ref, start=None, shifted=None, place_ref=None):
    width = d3_ref.shape[2] // 128
    for r in range(8):
        tile, col = (sec * 8 + r) // width, ((sec * 8 + r) % width) * 128
        cols = slice(col, col + 128)
        here = slice(r * 128, (r + 1) * 128)
        prior = ref[0:MEMBERS, here]
        mean = jnp.sum(prior, axis=0, keepdims=True) / MEMBERS
        dev = prior - mean
        spread = jnp.sum(dev * dev, axis=0, keepdims=True) / (MEMBERS - 1)
        value = ref[VALUE : VALUE + 1, here]
        error = ref[ERROR : ERROR + 1, here]
        place = ref[PLACE : PLACE + 1, here].astype(jnp.int32)
        total = spread + error
        scale = 1.0 / (total * (MEMBERS - 1))
        shrink = 1.0 / (1.0 + jnp.sqrt(error / total))
        step = (value - mean) - shrink * dev
        high, low = split(dev)
        d3_ref[tile, 0:80, cols] = high
        d3_ref[tile, 80:160, cols] = high
        d3_ref[tile, 160:240, cols] = low
        d3_ref[tile, 240:256, cols] = jnp.zeros((16, 128), bf16)
        high, low = split(step)
        pad = jnp.zeros((48, 128), bf16)
        a2_ref[tile, 0:80, cols] = high
        a2_ref[tile, 80:128, cols] = pad
        a2_ref[tile, 128:208, cols] = low
        a2_ref[tile, 208:256, cols] = pad
        full = (8, 128)
        table = ref[TABLE : TABLE + BINS, here] * scale
        if shifted is None:
            first = start - place
            rising = first >= 0
            dist = jnp.abs(first)
            bin0 = dist >> BIN_BITS
            inner = dist & ((1 << BIN_BITS) - 1)
            turn = jnp.where(rising, (1 << BIN_BITS) - inner, inner + 1)
            bin1 = jnp.where(rising, bin0 + 1, jnp.maximum(bin0 - 1, 0))
            level = lax.broadcasted_iota(jnp.int32, full, 0)
            before = jnp.sum(jnp.where(level == bin0, table, 0.0), axis=0, keepdims=True)
            after = jnp.sum(jnp.where(level == bin1, table, 0.0), axis=0, keepdims=True)
            rows_ref[tile, 0:8, cols] = jnp.broadcast_to(turn.astype(f32), full)
            rows_ref[tile, 8:16, cols] = jnp.broadcast_to(before, full)
            rows_ref[tile, 16:24, cols] = jnp.broadcast_to(after, full)
        else:
            place_ref[tile, :, cols] = jnp.broadcast_to(shifted(place), full)
            rows_ref[tile, :, cols] = table


def add_gains(rows, weight, cov, a2_ref, tile, acc_ref):
    gain = (weight * cov).reshape(cov.shape[0] * 8, cov.shape[2])
    high, low = split(gain)
    nt = (((1,), (1,)), ((), ()))
    acc_ref[rows, :] += lax.dot_general(high, a2_ref[tile], nt, preferred_element_type=f32)
    acc_ref[rows, :128] += lax.dot_general(low, a2_ref[tile, 0:128, :], nt, preferred_element_type=f32)


def scattered(tile, dist_of, masked, e3_ref, posb_ref, d3_ref, a2_ref, rows_ref, place_ref, acc_ref):
    part = 256
    width = d3_ref.shape[2]
    for ic in range(CELLS // part):
        rows = slice(ic * part, (ic + 1) * part)
        cov = jnp.dot(e3_ref[rows, :], d3_ref[tile], preferred_element_type=f32).reshape(part // 8, 8, width)
        groups = []
        for h in range(width // 128):
            cols = slice(h * 128, (h + 1) * 128)
            place = place_ref[tile, :, cols]
            table = rows_ref[tile, :, cols]
            slabs = []
            for g in range(part // 8):
                at = ic * part + g * 8
                level = dist_of(posb_ref[at : at + 8, :], place) >> BIN_BITS
                if masked:
                    got = jnp.take_along_axis(table, level & (BINS - 1), axis=0, mode="promise_in_bounds")
                    got = jnp.where(level < BINS, got, 0.0)
                else:
                    got = jnp.take_along_axis(table, level, axis=0, mode="promise_in_bounds")
                slabs.append(got[None])
            groups.append(jnp.concatenate(slabs, axis=0))
        add_gains(rows, jnp.concatenate(groups, axis=2), cov, a2_ref, tile, acc_ref)


def place_cells(par_ref, posb_ref, sign):
    for r in range(8):
        row = jnp.broadcast_to(par_ref[18:19, r * 128 : (r + 1) * 128], (128, 128))
        posb_ref[r * 128 : (r + 1) * 128, :] = row.T.astype(jnp.int32) * sign


def replay_kernel(
    at_ref, par_ref, x_ref, own_ref, side_ref, off_ref, out_ref,
    e3_ref, posb_ref, acc_ref, d3_ref, a2_ref, rows_ref, place_ref
):
    sign = at_ref[1]
    prepare_cells(x_ref, e3_ref)
    place_cells(par_ref, posb_ref, sign)
    work = (e3_ref, posb_ref, d3_ref, a2_ref, rows_ref, place_ref, acc_ref)
    sections = (
        (own_ref, lambda place: place * sign),
        (side_ref, lambda place: place * sign + BLOCK),
        (off_ref, lambda place: place * sign - BLOCK),
    )
    for sec, (ref, shifted) in enumerate(sections):
        prepare_section(sec, ref, d3_ref, a2_ref, rows_ref, shifted=shifted, place_ref=place_ref)
    acc_ref[...] = jnp.zeros_like(acc_ref)
    scattered(0, lambda pos, place: jnp.abs(pos - place), False, *work)
    scattered(1, lambda pos, place: place - pos, True, *work)
    scattered(2, lambda pos, place: pos - place, True, *work)
    finish(x_ref, acc_ref, out_ref)
    out_ref[MEMBERS:BUNDLE, :] = par_ref[16:32, :]


def replay(kernel, sections, name, at, par, *arrays):
    return pl.pallas_call(
        kernel,
        out_shape=jax.ShapeDtypeStruct((BUNDLE, CELLS), f32),
        in_specs=[SM, VM] + [VM] * len(arrays),
        out_specs=VM,
        scratch_shapes=[
            pltpu.VMEM((CELLS, 256), bf16),
            pltpu.VMEM((CELLS, 128), jnp.int32),
            pltpu.VMEM((CELLS, 256), f32),
            pltpu.VMEM((sections, 256, 1024), bf16),
            pltpu.VMEM((sections, 256, 1024), bf16),
            pltpu.VMEM((sections, 8, 1024), f32),
            pltpu.VMEM((sections, 8, 1024), jnp.int32),
        ],
        compiler_params=PARAMS,
        cost_estimate=pl.CostEstimate(flops=4_000_000_000 * sections, bytes_accessed=2_000_000, transcendentals=0),
        name=name,
    )(at, par, *arrays)


def finish(x_ref, acc_ref, out_ref, strided=False):
    for r in range(8):
        rows = slice(r * 128, (r + 1) * 128)
        step = (acc_ref[rows, :128] + acc_ref[rows, 128:]).T
        value = x_ref[:, rows] + step[:MEMBERS, :]
        if strided:
            out_ref[pl.ds(r, MEMBERS, stride=8), :] = value
        else:
            out_ref[0:MEMBERS, rows] = value


def update_kernel(
    last, at_ref, cells_ref, own_ref, side_ref, off_ref, out_ref, x_ref, e3_ref, d3_ref, a2_ref, rows_ref, acc_ref
):
    start, sign = at_ref[0], at_ref[1]
    if last:
        x_ref = cells_ref
    else:
        for r in range(8):
            x_ref[:, r * 128 : (r + 1) * 128] = cells_ref[pl.ds(r, MEMBERS, stride=8), :]
    prepare_cells(x_ref, e3_ref)
    sections = ((own_ref, start), (side_ref, start - sign * BLOCK), (off_ref, start + sign * BLOCK))
    for sec, (ref, first) in enumerate(sections):
        prepare_section(sec, ref, d3_ref, a2_ref, rows_ref, start=first)
    acc_ref[...] = jnp.zeros_like(acc_ref)
    tiles, _, width = d3_ref.shape
    part = CELLS

    def tile_step(tile, carry):
        for ic in range(CELLS // part):
            rows = slice(ic * part, (ic + 1) * part)
            shape = (part // 8, 8, width)
            cov = jnp.dot(e3_ref[rows, :], d3_ref[tile], preferred_element_type=f32).reshape(shape)
            at = lax.broadcasted_iota(jnp.int32, (part, width), 0).astype(f32).reshape(shape) + float(ic * part)
            turn = rows_ref[tile, 0:8, :][None]
            weight = jnp.where(at >= turn, rows_ref[tile, 16:24, :][None], rows_ref[tile, 8:16, :][None])
            add_gains(rows, weight, cov, a2_ref, tile, acc_ref)
        return carry

    lax.fori_loop(0, tiles, tile_step, 0, unroll=tiles)
    finish(x_ref, acc_ref, out_ref, strided=last)


def update(last, at, x, own, side, off):
    def kernel(*refs):
        update_kernel(last, *refs)

    width = 768
    tiles = MERGED // width
    return pl.pallas_call(
        kernel,
        out_shape=jax.ShapeDtypeStruct((ROWS, 128) if last else (MEMBERS, CELLS), f32),
        in_specs=[SM, VM, VM, VM, VM],
        out_specs=VM,
        scratch_shapes=[
            pltpu.VMEM((MEMBERS, CELLS), f32),
            pltpu.VMEM((CELLS, 256), bf16),
            pltpu.VMEM((tiles, 256, width), bf16),
            pltpu.VMEM((tiles, 256, width), bf16),
            pltpu.VMEM((tiles, 24, width), f32),
            pltpu.VMEM((CELLS, 256), f32),
        ],
        compiler_params=PARAMS,
        cost_estimate=pl.CostEstimate(flops=9_000_000_000, bytes_accessed=2_000_000, transcendentals=0),
        name="update_last" if last else "update_first",
    )(at, x, own, side, off)


def unsend_kernel(x_ref, out_ref):
    for c in range(128):
        d, r = c // 8, c % 8
        out_ref[:, c * 128 : (c + 1) * 128] = x_ref[pl.ds(d * 40 + r, 5, stride=8), :]


def unsend(x):
    return pl.pallas_call(
        unsend_kernel,
        out_shape=jax.ShapeDtypeStruct((5, BLOCK), f32),
        in_specs=[VM],
        out_specs=VM,
        compiler_params=PARAMS,
        name="unsend",
    )(x)


def per_device(samples, quantity, variance, grid_point, sort, tab):
    count = lax.axis_size("space")
    space = lax.axis_index("space")
    member = lax.axis_index("member")
    swap = [(i, i ^ 1) for i in range(count)]
    hop = [(i, (i + (1 if i % 2 else -1)) % count) for i in range(count)]
    odd = space % 2
    at = jnp.stack([member * CELLS, 1 - 2 * odd]).astype(jnp.int32)

    send, picks, par = pick(samples, quantity, variance, grid_point, sort, tab)
    gathered = lax.all_gather(picks, "member", axis=0).reshape(2 * ROWS, 128)
    own, second = make_bundle(gathered, par)
    send, own = lax.optimization_barrier((send, own))
    cells = lax.all_to_all(send.reshape(16, 40, 128), "member", 0, 0, tiled=True).reshape(ROWS, 128)
    off = lax.ppermute(own, "space", hop)
    side = lax.ppermute(own, "space", swap)
    own2 = replay(replay_kernel, 3, "replay", at, par, second, own, side, off)
    off2 = lax.ppermute(own2, "space", hop)
    side2 = lax.ppermute(own2, "space", swap)
    cells = update(False, at, cells, own, side, off)
    cells = update(True, at, cells, own2, side2, off2)
    back = lax.all_to_all(cells.reshape(16, 40, 128), "member", 0, 0, tiled=True)
    return unsend(back.reshape(ROWS, 128))


def solution(mesh):
    in_specs = (
        P("member", "space"),
        P(None, "space"),
        P(None, "space"),
        P(None, "space"),
        P(None, "space"),
        P(),
    )
    return jax.shard_map(
        per_device, mesh=mesh, in_specs=in_specs, out_specs=P("member", "space"), check_vma=False
    )
```
